32 devices in a mesh: mem: 4 (over y, x), lat: 8 (over z, core).
Axes of the slice: x: 2, y: 2, z: 4, core: 2. Of those that a mesh axis runs over, the one named last changes fastest.
Arguments:
- cotangent: bfloat16 [4, 3, 4, 1024, 4096], P('mem', None, None, 'lat'), may hold values from -6 to 6
- legendre: bfloat16 [704, 2, 352, 512], P('lat', None, None, 'mem'), may hold values from -0.25 to 0.25
- wave_order: int32 [704], replicated, may hold values from 0 to 703, each once
- mode_depth: float32 [4], replicated, may hold values from 0.5 to 20
- diffusion: float32 [4], replicated, may hold values from 0.5 to 8
- quad_weights: float32 [512], replicated, may hold values from 0.25 to 2.5
Outputs:
- adjoint: bfloat16 [4, 3, 4, 1024, 4096], P('mem', None, None, 'lat')
The draws below stay inside these ranges and needn't reach their ends.
Inputs may be any that keep to these rules, and one draw needn't show every extreme that they name: `wave_order`: each zonal wavenumber 0 to 703 appears exactly once; legendre's first index follows this order.
All inputs are finite; a program needn't handle non-finite values.
Results may differ from the reference program's by a relative error of at most 0.0076.
Values may be sent and summed in bfloat16 or wider, within the bound.
A program may use at most 192 MiB of HBM per device.

```python
import math
import jax
import jax.numpy as jnp
from jax import lax

NLON = 4096
NLAT = 1024
WAVES = 704
DEGREES = 704
MODES = 4
MEMBERS = 4
NLATH = 512


def steps_of(stream_key, shape, cuts, least, high):
    factor_of = 1.0
    for dim, parts in cuts:
        steps = jax.random.uniform(jax.random.fold_in(jax.random.fold_in(stream_key, 6), dim), (parts,), jnp.float32, least / len(cuts), high / len(cuts))
        factor_of = factor_of * jnp.repeat(jnp.exp(steps), shape[dim] // parts).reshape((-1,) + (1,) * (len(shape) - 1 - dim))
    return factor_of


def centred(stream_key, extent, deviation, most, split=(), kind=jnp.bfloat16):
    drawn = deviation * jax.random.normal(stream_key, extent, jnp.float32)
    if split:
        drawn = drawn * steps_of(stream_key, extent, split, -0.22, 0.18)
    return jnp.clip(drawn, -most, most).astype(kind)


def setup_inputs(seed: int = 0) -> dict:
    key_list = jax.random.split(jax.random.key(seed), 7)
    return {
        "cotangent": centred(key_list[0], (MEMBERS, 3, MODES, NLAT, NLON), 1.0, 6.0, ((0, 4), (3, 8))),
        "legendre": centred(key_list[1], (WAVES, 2, DEGREES // 2, NLATH), NLATH ** -0.5, 0.25, ((0, 8), (3, 4))),
        "wave_order": jax.random.permutation(key_list[2], WAVES).astype(jnp.int32),
        "mode_depth": jnp.clip(jnp.exp(jax.random.uniform(key_list[3], (MODES,), jnp.float32, math.log(0.5), math.log(20.0))), 0.5, 20.0),
        "diffusion": jnp.clip(jnp.exp(jax.random.uniform(key_list[4], (MODES,), jnp.float32, math.log(0.5), math.log(8.0))), 0.5, 8.0),
        "quad_weights": jnp.clip(jnp.exp(jax.random.uniform(key_list[5], (NLATH,), jnp.float32, math.log(0.25), math.log(2.5))), 0.25, 2.5),
    }


def fourier_table(wave_order, lon_count):
    wave_ids = jnp.repeat(wave_order, 2)
    parity = jnp.arange(wave_ids.shape[0], dtype=jnp.int32) % 2
    longitude = jnp.arange(lon_count, dtype=jnp.int32)[:, None]
    phases = (longitude * wave_ids[None, :]) % lon_count
    angles = phases.astype(jnp.float32) * jnp.float32(2.0 * math.pi / lon_count)
    values = jnp.where(parity[None, :] == 0, jnp.cos(angles), -jnp.sin(angles))
    return values.astype(jnp.bfloat16), wave_ids


def implicit(spectral, degree, top_degree, mode_depth, diffusion):
    count_waves, half_deg, pieces, channels = spectral.shape
    levels = mode_depth.shape[0]
    values = spectral.reshape(count_waves, half_deg, pieces, 3, levels)
    degree_f = degree.astype(jnp.float32)
    scaled = (degree_f * (degree_f + 1.0) / (top_degree * (top_degree + 1.0)))[:, :, None, None]
    vorticity = values[:, :, :, 0] / (1.0 + diffusion * scaled * scaled)
    damping = 1.0 / (1.0 + mode_depth * scaled)
    divergence = damping * (values[:, :, :, 1] - mode_depth * values[:, :, :, 2])
    height = damping * (scaled * values[:, :, :, 1] + values[:, :, :, 2])
    joined = jnp.stack([vorticity, divergence, height], axis=3)
    return joined.reshape(count_waves, half_deg, pieces, channels).astype(jnp.bfloat16)


def widen(values):
    return lax.optimization_barrier(values).astype(jnp.float32)


def one_member(member_field, legendre, wave_order, mode_depth, diffusion, quad_weights):
    highest = lax.Precision.HIGHEST
    fields, levels, lat_count, lon_count = member_field.shape
    half_lat = lat_count // 2
    total_waves = wave_order.shape[0]
    half_deg = legendre.shape[2]
    channels = fields * levels
    fourier, wave_ids = fourier_table(wave_order, lon_count)
    table_wide = fourier.astype(jnp.float32)
    flattened = member_field.reshape(channels * lat_count, lon_count).astype(jnp.float32)
    coeffs = jnp.dot(flattened, table_wide, precision=highest)
    factor = jnp.where(wave_ids == 0, 1.0, 2.0).astype(jnp.float32)
    coeffs = (coeffs * factor[None, :]).astype(jnp.bfloat16)
    coeffs = widen(coeffs).T.reshape(total_waves, 2, channels, lat_count)
    northern = coeffs[..., :half_lat]
    southern = coeffs[..., half_lat:]
    even_part = widen((northern + southern).astype(jnp.bfloat16))
    odd_part = widen((northern - southern).astype(jnp.bfloat16))
    basis_wide = legendre.astype(jnp.float32)
    analysed_even = jnp.einsum("mil,mqcl->miqc", basis_wide[:, 0], even_part, precision=highest)
    analysed_odd = jnp.einsum("mil,mqcl->miqc", basis_wide[:, 1], odd_part, precision=highest)
    degree_base = 2 * jnp.arange(half_deg, dtype=jnp.int32)[None, :] + wave_order[:, None]
    top_degree = float(total_waves + 2 * half_deg - 2)
    spectral_even = widen(implicit(analysed_even, degree_base, top_degree, mode_depth, diffusion))
    spectral_odd = widen(implicit(analysed_odd, degree_base + 1, top_degree, mode_depth, diffusion))
    synth_even = jnp.einsum("mil,miqc->mqcl", basis_wide[:, 0], spectral_even, precision=highest)
    synth_odd = jnp.einsum("mil,miqc->mqcl", basis_wide[:, 1], spectral_odd, precision=highest)
    weights = quad_weights[None, None, None, :]
    gridded = jnp.concatenate([weights * (synth_even + synth_odd), weights * (synth_even - synth_odd)], axis=3)
    gridded = widen(gridded.astype(jnp.bfloat16)).reshape(2 * total_waves, channels * lat_count)
    result = jnp.dot(gridded.T, table_wide.T, precision=highest) * (1.0 / lon_count)
    return result.astype(jnp.bfloat16).reshape(fields, levels, lat_count, lon_count)


def reference(cotangent, legendre, wave_order, mode_depth, diffusion, quad_weights):
    def single(member_field):
        return one_member(member_field, legendre, wave_order, mode_depth, diffusion, quad_weights)

    return lax.map(single, cotangent)
```

```python
import functools
import math

import jax
import jax.numpy as jnp
from jax import lax
from jax.experimental import pallas as pl
from jax.experimental.pallas import tpu as pltpu
from jax.sharding import PartitionSpec as P

CHUNKS = 2
AXES = ("lat", "mem")


def fourier_table(waves, lon_count):
    fine = 1 << ((lon_count.bit_length() - 1) // 2)
    coarse = lon_count // fine
    unit = jnp.float32(2.0 * math.pi / lon_count)
    ids = jnp.repeat(waves, 2)[None, :]
    is_cos = jnp.arange(ids.shape[1], dtype=jnp.int32)[None, :] % 2 == 0
    high = (jnp.arange(coarse, dtype=jnp.int32)[:, None] * fine * ids % lon_count).astype(jnp.float32) * unit
    low = (jnp.arange(fine, dtype=jnp.int32)[:, None] * ids % lon_count).astype(jnp.float32) * unit
    cos_high, sin_high = jnp.cos(high), jnp.sin(high)
    first = jnp.where(is_cos, cos_high, -sin_high)
    second = jnp.where(is_cos, sin_high, cos_high)
    first, second, cos_low, sin_low = lax.optimization_barrier((first, second, jnp.cos(low), jnp.sin(low)))
    values = first[:, None] * cos_low[None] - second[:, None] * sin_low[None]
    return lax.optimization_barrier(values.astype(jnp.bfloat16).reshape(lon_count, ids.shape[1]))


def spectral_kernel(
    fields, top_degree, waves_ref, coeff_ref, legendre_ref, depth_ref, diffusion_ref, weight_ref, out_ref
):
    bands, members, _, rows, width = coeff_ref.shape
    parts = legendre_ref.shape[0]
    half_deg = legendre_ref.shape[3]
    half = bands // 2
    piece = rows // fields
    group = members * piece
    wave = waves_ref[pl.program_id(0)]
    depth, diffusion, weight = depth_ref[...], diffusion_ref[...], weight_ref[...]

    def by_field(values):
        return jnp.concatenate(
            [values[e, f * piece : (f + 1) * piece] for f in range(fields) for e in range(members)], axis=0
        )

    evens, odds = [], []
    for b in range(half):
        north = coeff_ref[b, :, 0].astype(jnp.float32)
        south = coeff_ref[half + b, :, 0].astype(jnp.float32)
        evens.append(by_field(north + south).astype(jnp.bfloat16))
        odds.append(by_field(north - south).astype(jnp.bfloat16))
    synth = []
    for p, blocks in enumerate((evens, odds)):
        grid_rows = jnp.concatenate(blocks, axis=1)
        basis = jnp.concatenate([legendre_ref[s, 0, p] for s in range(parts)], axis=1)
        analysed = lax.dot_general(
            grid_rows, basis, (((1,), (1,)), ((), ())), preferred_element_type=jnp.float32
        )
        degree = 2 * lax.broadcasted_iota(jnp.int32, (1, half_deg), 1) + (wave + p)
        degree = degree.astype(jnp.float32)
        scaled = degree * (degree + 1.0) / (top_degree * (top_degree + 1.0))
        damping = 1.0 / (1.0 + depth * scaled)
        vor, div, hgt = (analysed[f * group : (f + 1) * group] for f in range(3))
        spectral = jnp.concatenate(
            [
                vor / (1.0 + diffusion * scaled * scaled),
                damping * (div - depth * hgt),
                damping * (scaled * div + hgt),
            ],
            axis=0,
        ).astype(jnp.bfloat16)
        synth.append(jnp.dot(spectral, basis, preferred_element_type=jnp.float32))
    both = (weight * (synth[0] + synth[1]), weight * (synth[0] - synth[1]))
    for side, values in enumerate(both):
        for b in range(half):
            block = values[:, b * width : (b + 1) * width]
            for e in range(members):
                out_ref[side * half + b, e, 0] = jnp.concatenate(
                    [block[f * group + e * piece : f * group + (e + 1) * piece] for f in range(fields)], axis=0
                ).astype(jnp.bfloat16)


def spectral_step(fields, top_degree, waves, coeffs, basis, depth, diffusion, weights):
    bands, members, count, rows, width = coeffs.shape
    parts, _, _, half_deg, lats = basis.shape
    whole = lambda array: pl.BlockSpec(array.shape, lambda m, waves: (0, 0))
    block = pl.BlockSpec((bands, members, 1, rows, width), lambda m, waves: (0, 0, m, 0, 0))
    flops = 8 * count * half_deg * lats * parts * members * rows
    return pl.pallas_call(
        functools.partial(spectral_kernel, fields, top_degree),
        grid_spec=pltpu.PrefetchScalarGridSpec(
            num_scalar_prefetch=1,
            grid=(count,),
            in_specs=[
                block,
                pl.BlockSpec((parts, 1, 2, half_deg, lats), lambda m, waves: (0, m, 0, 0, 0)),
                whole(depth),
                whole(diffusion),
                whole(weights),
            ],
            out_specs=block,
        ),
        out_shape=jax.ShapeDtypeStruct(coeffs.shape, jnp.bfloat16),
        compiler_params=pltpu.CompilerParams(vmem_limit_bytes=40 * 1024 * 1024),
        cost_estimate=pl.CostEstimate(
            flops=flops, bytes_accessed=2 * (basis.size + 2 * coeffs.size), transcendentals=0
        ),
    )(waves, coeffs, basis, depth, diffusion, weights)


def shards(cotangent, legendre, wave_order, mode_depth, diffusion, quad_weights):
    members, fields, levels, band_rows, lon_count = cotangent.shape
    lat_count, mem_count = lax.axis_size("lat"), lax.axis_size("mem")
    devices = lat_count * mem_count
    total_waves = wave_order.shape[0]
    lat_waves = total_waves // lat_count
    own_count = -(-lat_waves // mem_count)
    extra = own_count * mem_count - lat_waves
    half_deg = legendre.shape[2]
    channels = fields * levels
    rows = 2 * channels
    top_degree = float(total_waves + 2 * half_deg - 2)

    waves = jnp.pad(wave_order.reshape(lat_count, lat_waves), ((0, 0), (0, extra)))
    waves = waves.reshape(lat_count, mem_count, own_count)
    own_waves = waves[lax.axis_index("lat"), lax.axis_index("mem")]
    if extra:
        legendre = jnp.pad(legendre, ((0, extra), (0, 0), (0, 0), (0, 0)))
    legendre = legendre.reshape((mem_count, own_count) + legendre.shape[1:])
    step = -(-own_count // CHUNKS)
    cuts = [(lo, min(lo + step, own_count)) for lo in range(0, own_count, step)]

    flattened = cotangent.reshape(channels * band_rows, lon_count)
    depth = jnp.tile(mode_depth, mem_count * 2 * members)[:, None]
    spread = jnp.tile(diffusion, mem_count * 2 * members)[:, None]
    weights = quad_weights[None, :]

    tables, bases, received = [], [], []
    for lo, hi in cuts:
        part = legendre[:, lo:hi]
        if bases:
            part = lax.optimization_barrier((part, bases[-1]))[0]
        bases.append(lax.all_to_all(part, "mem", split_axis=0, concat_axis=0, tiled=True))
    for lo, hi in cuts:
        ids = waves[:, :, lo:hi].reshape(-1)
        table = fourier_table(ids, lon_count)
        tables.append(table)
        coeffs = lax.dot_general(
            table, flattened, (((0,), (1,)), ((), ())), preferred_element_type=jnp.float32
        )
        factor = jnp.where(jnp.repeat(ids, 2) == 0, 1.0, 2.0).astype(jnp.float32)
        coeffs = (coeffs * factor[:, None]).astype(jnp.bfloat16)
        coeffs = coeffs.reshape(devices, hi - lo, 2, fields, levels, band_rows)
        coeffs = jnp.transpose(coeffs, (0, 1, 3, 2, 4, 5)).reshape(devices, hi - lo, rows, band_rows)
        received.append(lax.all_to_all(coeffs, AXES, split_axis=0, concat_axis=0, tiled=True))
    total = None
    for (lo, hi), table, basis, coeffs in zip(cuts, tables, bases, received):
        shape = (lat_count, mem_count, hi - lo, rows, band_rows)
        gridded = spectral_step(
            fields, top_degree, own_waves[lo:hi], coeffs.reshape(shape), basis, depth, spread, weights
        )
        returned = lax.all_to_all(gridded.reshape(coeffs.shape), AXES, split_axis=0, concat_axis=0, tiled=True)
        returned = returned.reshape(devices, hi - lo, fields, 2, levels, band_rows)
        returned = jnp.transpose(returned, (0, 1, 3, 2, 4, 5)).reshape(-1, channels * band_rows)
        product = lax.dot_general(
            returned, table, (((0,), (1,)), ((), ())), preferred_element_type=jnp.float32
        )
        total = product if total is None else total + product
    result = (total * jnp.float32(1.0 / lon_count)).astype(jnp.bfloat16)
    return result.reshape(members, fields, levels, band_rows, lon_count)


def solution(mesh):
    placed = (P("mem", None, None, "lat", None), P("lat", None, None, "mem"), P(), P(), P(), P())
    return jax.shard_map(
        shards,
        mesh=mesh,
        in_specs=placed,
        out_specs=P("mem", None, None, "lat", None),
        check_vma=False,
    )
```

```python
import functools
import math

import jax
import jax.numpy as jnp
from jax import lax
from jax.experimental import pallas as pl
from jax.experimental.pallas import tpu as pltpu
from jax.sharding import PartitionSpec as P

CHUNKS = 3
AXES = ("lat", "mem")


def fourier_table(waves, lon_count):
    fine = 1 << ((lon_count.bit_length() - 1) // 2)
    coarse = lon_count // fine
    unit = jnp.float32(2.0 * math.pi / lon_count)
    ids = jnp.repeat(waves, 2)[None, :]
    is_cos = jnp.arange(ids.shape[1], dtype=jnp.int32)[None, :] % 2 == 0
    high = (jnp.arange(coarse, dtype=jnp.int32)[:, None] * fine * ids % lon_count).astype(jnp.float32) * unit
    low = (jnp.arange(fine, dtype=jnp.int32)[:, None] * ids % lon_count).astype(jnp.float32) * unit
    cos_high, sin_high = jnp.cos(high), jnp.sin(high)
    first = jnp.where(is_cos, cos_high, -sin_high)
    second = jnp.where(is_cos, sin_high, cos_high)
    first, second, cos_low, sin_low = lax.optimization_barrier((first, second, jnp.cos(low), jnp.sin(low)))
    values = first[:, None] * cos_low[None] - second[:, None] * sin_low[None]
    return lax.optimization_barrier(values.astype(jnp.bfloat16).reshape(lon_count, ids.shape[1]))


def zero_after(array):
    first = array[(0,) * array.ndim]
    return (first != first).astype(jnp.int32)


def spectral_kernel(
    fields, top_degree, scalars_ref, coeff_ref, depth_ref, diffusion_ref, weight_ref, own_ref, *refs
):
    *legendre_refs, out_ref = refs
    bands, members, _, rows, width = coeff_ref.shape
    half_deg, lats = own_ref.shape[3:]
    parts = 1 + len(legendre_refs)
    half = bands // 2
    piece = rows // fields
    group = members * piece
    wave = scalars_ref[1 + pl.program_id(0)]
    per_part = lats // width
    order = [(scalars_ref[0] ^ k) * per_part + t for k in range(parts) for t in range(per_part)]
    depth, diffusion, weight = depth_ref[...], diffusion_ref[...], weight_ref[...]

    def by_field(values):
        return jnp.concatenate(
            [values[e, f * piece : (f + 1) * piece] for f in range(fields) for e in range(members)], axis=0
        )

    evens, odds = [], []
    for b in order:
        north = coeff_ref[b, :, 0].astype(jnp.float32)
        south = coeff_ref[half + b, :, 0].astype(jnp.float32)
        evens.append(by_field(north + south).astype(jnp.bfloat16))
        odds.append(by_field(north - south).astype(jnp.bfloat16))
    synth = []
    for p, blocks in enumerate((evens, odds)):
        grid_rows = jnp.concatenate(blocks, axis=1)
        basis = jnp.concatenate([own_ref[0, 0, p]] + [ref[0, p] for ref in legendre_refs], axis=1)
        analysed = lax.dot_general(
            grid_rows, basis, (((1,), (1,)), ((), ())), preferred_element_type=jnp.float32
        )
        degree = 2 * lax.broadcasted_iota(jnp.int32, (1, half_deg), 1) + (wave + p)
        degree = degree.astype(jnp.float32)
        scaled = degree * (degree + 1.0) / (top_degree * (top_degree + 1.0))
        damping = 1.0 / (1.0 + depth * scaled)
        vor, div, hgt = (analysed[f * group : (f + 1) * group] for f in range(3))
        spectral = jnp.concatenate(
            [
                vor / (1.0 + diffusion * scaled * scaled),
                damping * (div - depth * hgt),
                damping * (scaled * div + hgt),
            ],
            axis=0,
        ).astype(jnp.bfloat16)
        synth.append(jnp.dot(spectral, basis, preferred_element_type=jnp.float32))
    both = (weight * (synth[0] + synth[1]), weight * (synth[0] - synth[1]))
    for side, values in enumerate(both):
        for place, b in enumerate(order):
            block = values[:, place * width : (place + 1) * width]
            for e in range(members):
                out_ref[side * half + b, e, 0] = jnp.concatenate(
                    [block[f * group + e * piece : f * group + (e + 1) * piece] for f in range(fields)], axis=0
                ).astype(jnp.bfloat16)


def spectral_step(fields, top_degree, start, scalars, coeffs, own, bases, depth, diffusion, weights):
    bands, members, count, rows, width = coeffs.shape
    half_deg, lats = own.shape[3:]
    parts = 1 + len(bases)
    whole = lambda array: pl.BlockSpec(array.shape, lambda m, scalars: (0, 0))
    block = pl.BlockSpec((bands, members, 1, rows, width), lambda m, scalars: (0, 0, m, 0, 0))
    arrived = pl.BlockSpec((1, 2, half_deg, lats), lambda m, scalars: (m, 0, 0, 0))
    held = pl.BlockSpec((1, 1, 2, half_deg, lats), lambda m, scalars: (scalars[0], start + m, 0, 0, 0))
    basis_size = count * 2 * half_deg * lats * parts
    return pl.pallas_call(
        functools.partial(spectral_kernel, fields, top_degree),
        grid_spec=pltpu.PrefetchScalarGridSpec(
            num_scalar_prefetch=1,
            grid=(count,),
            in_specs=[block, whole(depth), whole(diffusion), whole(weights), held] + [arrived] * len(bases),
            out_specs=block,
        ),
        out_shape=jax.ShapeDtypeStruct(coeffs.shape, jnp.bfloat16),
        compiler_params=pltpu.CompilerParams(vmem_limit_bytes=40 * 1024 * 1024),
        cost_estimate=pl.CostEstimate(
            flops=4 * basis_size * members * rows,
            bytes_accessed=2 * (basis_size + 2 * coeffs.size),
            transcendentals=0,
        ),
    )(scalars, coeffs, depth, diffusion, weights, own, *bases)


def shards(cotangent, legendre, wave_order, mode_depth, diffusion, quad_weights):
    members, fields, levels, band_rows, lon_count = cotangent.shape
    lat_count, mem_count = lax.axis_size("lat"), lax.axis_size("mem")
    devices = lat_count * mem_count
    total_waves = wave_order.shape[0]
    lat_waves = total_waves // lat_count
    own_count = -(-lat_waves // mem_count)
    extra = own_count * mem_count - lat_waves
    half_deg = legendre.shape[2]
    channels = fields * levels
    rows = 2 * channels
    top_degree = float(total_waves + 2 * half_deg - 2)

    waves = jnp.pad(wave_order.reshape(lat_count, lat_waves), ((0, 0), (0, extra)))
    waves = waves.reshape(lat_count, mem_count, own_count)
    me = lax.axis_index("mem")
    own_waves = waves[lax.axis_index("lat"), me]
    if extra:
        legendre = jnp.pad(legendre, ((0, extra), (0, 0), (0, 0), (0, 0)))
    legendre = legendre.reshape((mem_count, own_count) + legendre.shape[1:])
    step = -(-own_count // CHUNKS)
    cuts = [(lo, min(lo + step, own_count)) for lo in range(0, own_count, step)]

    flattened = cotangent.reshape(channels * band_rows, lon_count)
    depth = jnp.tile(mode_depth, mem_count * 2 * members)[:, None]
    spread = jnp.tile(diffusion, mem_count * 2 * members)[:, None]
    weights = quad_weights.reshape(mem_count, -1)[me ^ jnp.arange(mem_count)].reshape(1, -1)

    tables, bases, received = [], [], []
    for lo, hi in cuts:
        arrivals = []
        for k in range(1, mem_count):
            place = me ^ k
            if len(bases) > 1:
                place = place + zero_after(bases[-2][k - 1])
            part = lax.dynamic_slice_in_dim(legendre, place, 1)[0, lo:hi]
            arrivals.append(lax.ppermute(part, "mem", [(i, i ^ k) for i in range(mem_count)]))
        bases.append(arrivals)
    for lo, hi in cuts:
        ids = waves[:, :, lo:hi].reshape(-1)
        if tables:
            ids = ids + zero_after(coeffs)
        table = fourier_table(ids, lon_count)
        tables.append(table)
        coeffs = lax.dot_general(
            table, flattened, (((0,), (1,)), ((), ())), preferred_element_type=jnp.float32
        )
        factor = jnp.where(jnp.repeat(ids, 2) == 0, 1.0, 2.0).astype(jnp.float32)
        coeffs = (coeffs * factor[:, None]).astype(jnp.bfloat16)
        coeffs = coeffs.reshape(devices, hi - lo, 2, fields, levels, band_rows)
        coeffs = jnp.transpose(coeffs, (0, 1, 3, 2, 4, 5)).reshape(devices, hi - lo, rows, band_rows)
        received.append(lax.all_to_all(coeffs, AXES, split_axis=0, concat_axis=0, tiled=True))
    total = None
    for (lo, hi), table, basis, coeffs in zip(cuts, tables, bases, received):
        shape = (lat_count, mem_count, hi - lo, rows, band_rows)
        scalars = jnp.concatenate([me[None].astype(jnp.int32), own_waves[lo:hi]])
        gridded = spectral_step(
            fields, top_degree, lo, scalars, coeffs.reshape(shape), legendre, basis, depth, spread, weights
        )
        returned = lax.all_to_all(gridded.reshape(coeffs.shape), AXES, split_axis=0, concat_axis=0, tiled=True)
        returned = returned.reshape(devices, hi - lo, fields, 2, levels, band_rows)
        returned = jnp.transpose(returned, (0, 1, 3, 2, 4, 5)).reshape(-1, channels * band_rows)
        product = lax.dot_general(
            returned, table, (((0,), (1,)), ((), ())), preferred_element_type=jnp.float32
        )
        total = product if total is None else total + product
    result = (total * jnp.float32(1.0 / lon_count)).astype(jnp.bfloat16)
    return result.reshape(members, fields, levels, band_rows, lon_count)


def solution(mesh):
    placed = (P("mem", None, None, "lat", None), P("lat", None, None, "mem"), P(), P(), P(), P())
    return jax.shard_map(
        shards,
        mesh=mesh,
        in_specs=placed,
        out_specs=P("mem", None, None, "lat", None),
        check_vma=False,
    )
```
